512 devices in a mesh: stack: 16 (over y, x_lo, core), space: 32 (over x_hi, z).
Axes of the slice: x: 4 (x_hi: 2, x_lo: 2; x = x_hi * 2 + x_lo), y: 4, z: 16, core: 2. Of those that a mesh axis runs over, the one named last changes fastest.
Arguments:
- phases: float32 [576, 16, 32768], P('stack', None, 'space'), may hold values from -15 to 15
- pairs: int32 [576, 2], replicated, may hold values from 0 to 143, as said below
- ref_pixel: int32 [1], replicated, may hold values from 0 to 524287
- coherent: int32 [16, 32768], P(None, 'space'), may hold values 0 or 1
Outputs:
- screens: float32 [144, 32768], P('stack', 'space')
- residual: float32 [144, 16, 32768], P('stack', None, 'space')
The draws below stay inside these ranges and needn't reach their ends.
Inputs may be any that keep to these rules, and one draw needn't show every extreme that they name: `pairs`: each row holds an earlier and a later date, at most 8 dates apart; every two consecutive dates form a pair.
All inputs are finite; a program needn't handle non-finite values. No bound on the sum of `coherent` on one device may be relied on, other than what follows from the above.
Results may differ from the reference program's by a relative error of at most 0.00013.
Values sent between devices are 32-bit elements; how exact they have to be, the bound alone decides.
No kernel may reach another device: no remote copies, remote signals or barrier semaphores. Data moves between devices by JAX's collectives and lax.ppermute only.
A program may use at most 64 MiB of HBM per device.

```python
import math
import jax
import jax.numpy as jnp
from jax import lax

IFGS = 576
DATES = 144
ROWS = 16
COLS_DEV = 1024
SPAN = 8
TAU = 8
HALF = 256
COLS = 32768
N_SPACE = 32


def draw_phases(key, part):
    key = jax.random.fold_in(key, 11)
    subkeys = jax.random.split(key, 5)
    spread = jax.random.uniform(subkeys[0], (1, ROWS, COLS), jnp.float32, math.log(0.3), math.log(3.0))
    speckle = jnp.clip(jax.random.normal(subkeys[1], (IFGS, ROWS, COLS), jnp.float32), -4.0, 4.0)
    amplitude = 0.8 * jnp.clip(jax.random.normal(subkeys[2], (IFGS, 1, 1), jnp.float32), -3.0, 3.0)
    wavenumber = 2.0 * math.pi / (COLS_DEV * jax.random.uniform(subkeys[3], (IFGS, 1, 1), jnp.float32, 2.0, 8.0))
    offset = jax.random.uniform(subkeys[4], (IFGS, 1, 1), jnp.float32, -math.pi, math.pi)
    columns = jnp.arange(COLS, dtype=jnp.float32)[None, None, :]
    return jnp.exp(spread) * speckle + amplitude * jnp.sin(wavenumber * columns + offset)


def draw_pairs(key, part):
    key = jax.random.fold_in(key, 5)
    subkeys = jax.random.split(key, 3)
    chain_start = jnp.arange(DATES - 1, dtype=jnp.int32)
    extra_pairs = IFGS - DATES + 1
    date_gaps = jax.random.randint(subkeys[0], (extra_pairs,), 1, SPAN + 1, dtype=jnp.int32)
    starts = jax.random.randint(subkeys[1], (extra_pairs,), 0, 1 << 20, dtype=jnp.int32) % (DATES - date_gaps)
    earlier = jnp.concatenate([chain_start, starts])
    later_date = jnp.concatenate([chain_start + 1, starts + date_gaps])
    shuffle = jax.random.permutation(subkeys[2], IFGS)
    return jnp.stack([earlier[shuffle], later_date[shuffle]], axis=1).astype(jnp.int32)


def with_ends(drawn, stream_key, low, high):
    dims = drawn.shape
    place = [jax.random.randint(jax.random.fold_in(stream_key, axis), (), 0, dims[axis]) for axis in range(len(dims))]
    drawn = drawn.at[tuple(place)].set(low)
    longest = dims.index(max(dims))
    place[longest] = (place[longest] + 1) % dims[longest]
    return drawn.at[tuple(place)].set(high)


def setup_inputs(seed: int = 0) -> dict:
    splits = jax.random.split(jax.random.key(seed), 5)
    return {
        "phases": draw_phases(jax.random.fold_in(splits[4], 71), 0),
        "pairs": draw_pairs(jax.random.fold_in(splits[4], 71), 0),
        "ref_pixel": jax.random.randint(splits[2], (1,), 0, ROWS * COLS).astype(jnp.int32),
        "coherent": with_ends((jax.random.randint(splits[3], (ROWS, COLS), 0, 10) < 7).astype(jnp.int32), jax.random.fold_in(splits[3], 1), 0, 1),
    }


def design(pairs):
    date_ids = jnp.arange(DATES, dtype=jnp.int32)
    later_date = (pairs[:, 1:2] == date_ids[None, :]).astype(jnp.float32)
    earlier = (pairs[:, 0:1] == date_ids[None, :]).astype(jnp.float32)
    return later_date - earlier

def inverse(design_mat):
    normal = jnp.dot(design_mat.T.astype(jnp.float32), design_mat.astype(jnp.float32), precision=lax.Precision.HIGHEST, preferred_element_type=jnp.float32)
    normal = normal + jnp.eye(DATES, dtype=jnp.float32)
    factor = jnp.linalg.cholesky(normal)
    return jax.scipy.linalg.cho_solve((factor, True), design_mat.T)

def smoother():
    date_steps = jnp.arange(DATES, dtype=jnp.float32)
    date_gap = date_steps[:, None] - date_steps[None, :]
    kernel = jnp.exp(-date_gap * date_gap / (2.0 * TAU * TAU))
    return kernel / jnp.sum(kernel, axis=1, keepdims=True)

def reference(phases, pairs, ref_pixel, coherent):
    highest = lax.Precision.HIGHEST
    design_mat = design(pairs)
    inverse_op = inverse(design_mat)
    smooth = smoother()
    flattened = phases.reshape(IFGS, ROWS * COLS)
    ref_column = lax.dynamic_slice_in_dim(flattened, ref_pixel[0], 1, 1)
    flattened = flattened - ref_column

    def one_block(block_index):
        in_block = lax.dynamic_slice_in_dim(flattened, block_index * COLS_DEV, COLS_DEV, 1)
        series = jnp.dot(inverse_op.astype(jnp.float32), in_block.astype(jnp.float32), precision=highest, preferred_element_type=jnp.float32)
        modelled = jnp.dot(design_mat.astype(jnp.float32), series.astype(jnp.float32), precision=highest, preferred_element_type=jnp.float32)
        misfit = jnp.mean(jnp.square(in_block - modelled), axis=0)
        high_pass = series - jnp.dot(smooth.astype(jnp.float32), series.astype(jnp.float32), precision=highest, preferred_element_type=jnp.float32)
        return (high_pass, misfit)
    highs, misfits = lax.map(one_block, jnp.arange(ROWS * N_SPACE, dtype=jnp.int32))
    high_pass = jnp.moveaxis(highs, 0, 1).reshape(DATES, ROWS, COLS)
    misfit = misfits.reshape(ROWS, COLS)
    mask_f = coherent.astype(jnp.float32)
    weight = mask_f / (1.0 + misfit)
    weighted = jnp.einsum('mrc,rc->mc', high_pass, weight, precision=highest)
    weight_sum = jnp.sum(weight, axis=0)
    zero_val = jnp.zeros((), weighted.dtype)
    wide = 2 * HALF + 1
    box_num = lax.reduce_window(weighted, zero_val, lax.add, (1, wide), (1, 1), ((0, 0), (HALF, HALF)))
    box_den = lax.reduce_window(weight_sum, zero_val, lax.add, (wide,), (1,), ((HALF, HALF),))
    screens = box_num / (1.0 + box_den[None, :])
    residual = mask_f[None, :, :] * (high_pass - screens[:, None, :])
    return (screens, residual)
```

```python
import functools

import jax
import jax.numpy as jnp
from jax import lax
from jax.experimental import pallas as pl
from jax.experimental.pallas import tpu as pltpu
from jax.sharding import Mesh, PartitionSpec as P

IFGS = 576
DATES = 144
ROWS = 16
TAU = 8
HALF = 256
STACK = 16
OWN_IFGS = IFGS // STACK
OWN_DATES = DATES // STACK
COLS = 1024
SPACE = 32
SUB = 8
LANE = 128
GROUP = 16
OUT_ROWS = STACK * GROUP
SUMS = OWN_DATES + 1
PIECE = SUMS + GROUP // SUB
PIXELS = SUB * LANE
WIDE = 256

STACK_AXES = ("y", "x_lo", "core")
SPACE_AXES = ("x_hi", "z_hi", "z_lo")

F32 = jnp.float32
BF16 = jnp.bfloat16
HIGHEST = lax.Precision.HIGHEST
FILLS = 4
VMEM_LIMIT = 16 * 1024 * 1024
BIG_LIMIT = 60 * 1024 * 1024


def tile_of(piece):
    return (piece // 8) * SUB, (piece % 8) * LANE


def split2(value):
    first = value.astype(BF16)
    return first, (value - first.astype(F32)).astype(BF16)


def iota(shape, axis):
    return lax.broadcasted_iota(jnp.int32, shape, axis)


def full(memory_space=pltpu.VMEM):
    return pl.BlockSpec(memory_space=memory_space)


def pack_kernel(pixel_ref, space_ref, x_ref, out_ref, cand_ref, held, in_sems, out_sems):
    step = OWN_IFGS // FILLS
    fills, sends = [], []
    for i in range(FILLS):
        ifgs = pl.ds(i * step, step)
        fills.append(
            pltpu.make_async_copy(x_ref.at[ifgs], held.at[ifgs], in_sems.at[i])
        )
        fills[-1].start()
    for i in range(FILLS):
        ifgs = pl.ds(i * step, step)
        fills[i].wait()
        for piece in range(STACK):
            r, c = tile_of(piece)
            send = pltpu.make_async_copy(
                held.at[ifgs, pl.ds(r, SUB), pl.ds(c, LANE)],
                out_ref.at[piece, ifgs],
                out_sems.at[i, piece],
            )
            send.start()
            sends.append(send)
    flat = pixel_ref[0]
    row = flat // (SPACE * COLS)
    col = lax.rem(flat, COLS)
    row_tile = pl.multiple_of((row // SUB) * SUB, SUB)
    col_tile = pl.multiple_of((col // LANE) * LANE, LANE)
    is_owner = space_ref[0] == lax.rem(flat, SPACE * COLS) // COLS
    picked = held[:, pl.ds(row_tile, SUB), pl.ds(col_tile, LANE)]
    shape = (OWN_IFGS, SUB, LANE)
    here = (iota(shape, 1) == lax.rem(row, SUB)) & (iota(shape, 2) == lax.rem(col, LANE))
    here = here & is_owner
    picked = jnp.sum(jnp.where(here, picked, 0.0), axis=1)
    picked = jnp.concatenate([picked, jnp.zeros((LANE - OWN_IFGS, LANE), F32)], axis=0)
    rows = lax.dot_general(
        jnp.ones((SUB, LANE), F32),
        picked,
        (((1,), (1,)), ((), ())),
        precision=HIGHEST,
        preferred_element_type=F32,
    )
    cand_ref[...] = rows[:1]
    for send in sends:
        send.wait()


def operator_kernel(pairs_ref, design_ref, design_t_ref, op_ref):
    dates = iota((DATES, IFGS), 0)
    later = (pairs_ref[1:2, :] == dates).astype(F32)
    earlier = (pairs_ref[0:1, :] == dates).astype(F32)
    design_t = later - earlier
    design_t_ref[...] = design_t.astype(BF16)
    design_ref[...] = jnp.concatenate([design_t.T] * 2, axis=1).astype(BF16)
    normal = lax.dot_general(
        design_t.astype(BF16),
        design_t.astype(BF16),
        (((1,), (1,)), ((), ())),
        preferred_element_type=F32,
    )
    eye = (iota((DATES, DATES), 0) == iota((DATES, DATES), 1)).astype(F32)
    normal = normal + eye
    diag = jnp.sum(normal * eye, axis=0, keepdims=True)
    error = eye - normal / diag
    inverse = eye / diag
    bound = 14.0 * jnp.max(diag)
    mul = functools.partial(jnp.dot, precision=HIGHEST, preferred_element_type=F32)

    def step(carry):
        power, inv, err = carry
        return power * 2.0, inv + mul(inv, err), mul(err, err)

    _, inverse, _ = lax.while_loop(
        lambda carry: carry[0] < bound, step, (jnp.float32(1.0), inverse, error)
    )
    inverse = inverse + mul(inverse, eye - mul(normal, inverse))
    steps = iota((DATES, DATES), 0) - iota((DATES, DATES), 1)
    gauss = jnp.exp(-(steps * steps).astype(F32) / (2.0 * TAU * TAU))
    smooth = gauss / jnp.sum(gauss, axis=1, keepdims=True)
    high = mul(eye - smooth, inverse)
    out_row = iota((OUT_ROWS, DATES), 0)
    place = out_row & (GROUP - 1)
    date = jnp.where(place < OWN_DATES, (out_row >> 4) * OWN_DATES + place, -1)
    spread = (iota((OUT_ROWS, DATES), 1) == date).astype(F32)
    first, second = split2(jnp.concatenate([inverse, mul(spread, high)], axis=0))
    op_ref[...] = jnp.concatenate([first, second, first], axis=1)


def invert_kernel(
    place_ref, x_ref, refs_ref, design_ref, design_t_ref, op_ref, mask_ref, high_ref, sums_ref
):
    place = place_ref[0]
    row_tile = pl.multiple_of((place // 8) * SUB, SUB)
    col_tile = pl.multiple_of(lax.rem(place, 8) * LANE, LANE)
    coherent = mask_ref[pl.ds(row_tile, SUB), pl.ds(col_tile, LANE)].astype(F32)
    is_weight = (iota((OUT_ROWS, LANE), 0) & (GROUP - 1)) == OWN_DATES
    ifg = iota((IFGS, STACK), 0)
    spread = (iota((IFGS, STACK), 1) == (ifg * 1821) >> 16).astype(F32)
    refs = refs_ref[:STACK] + refs_ref[STACK:]
    refs = jnp.dot(spread, refs, precision=HIGHEST, preferred_element_type=F32)
    ifg = iota((IFGS, LANE), 0)
    own = iota((IFGS, LANE), 1) == ifg - ((ifg * 1821) >> 16) * OWN_IFGS
    ref_phase = jnp.sum(jnp.where(own, refs, 0.0), axis=1, keepdims=True)
    rows_at_once = WIDE // LANE
    dot = functools.partial(jnp.dot, preferred_element_type=F32)
    sums = jnp.zeros((OUT_ROWS, LANE), F32)
    for first in range(0, SUB, rows_at_once):
        rows = range(first, first + rows_at_once)
        x = jnp.concatenate([x_ref[pl.ds(r, IFGS, stride=SUB), :] for r in rows], axis=1)
        x = x - ref_phase
        moment, moment_rest = split2(sum(dot(design_t_ref[...], term) for term in split2(x)))
        both = dot(op_ref[...], jnp.concatenate([moment, moment, moment_rest], axis=0))
        model = dot(design_ref[...], jnp.concatenate(split2(both[:DATES]), axis=0))
        gap = x - model
        misfit = jnp.sum(gap * gap, axis=0, keepdims=True) * (1.0 / IFGS)
        for i, r in enumerate(rows):
            part = slice(i * LANE, (i + 1) * LANE)
            weight = coherent[r : r + 1] / (1.0 + misfit[:, part])
            high = jnp.where(is_weight, 1.0, both[DATES:, part])
            weighted = high * weight
            sums = sums + weighted
            high = jnp.where(is_weight, weighted, high)
            high_ref[:, r * LANE : (r + 1) * LANE] = high
    sums_ref[...] = sums


def pieces_kernel(high_ref, sums_ref, out_ref):
    for r in range(SUB):
        for t in range(STACK):
            out_ref[pl.ds(t * PIECE * SUB + r, SUMS, stride=SUB), :] = high_ref[
                t * GROUP : t * GROUP + SUMS, r * LANE : (r + 1) * LANE
            ]
    for t in range(STACK):
        last = t * PIECE * SUB + SUMS * SUB
        out_ref[last : last + GROUP] = sums_ref[t * GROUP : (t + 1) * GROUP]


def screen_kernel(x_ref, mask_ref, screens_ref, residual_ref):
    halves = range(ROWS // SUB)
    tiles = COLS // LANE

    def own(c):
        total = 0.0
        for half in halves:
            piece = x_ref[half * tiles + c]
            weight = piece[OWN_DATES:SUMS]
            part = jnp.concatenate([piece[:OWN_DATES] * weight, weight], axis=0)
            total = total + part
        total = jnp.sum(total, axis=1)
        return jnp.concatenate([total, jnp.zeros((GROUP - SUMS, LANE), F32)], axis=0)

    def neighbour(c):
        total = sum(x_ref[half * tiles + c, SUMS:] for half in halves)
        return total.reshape(GROUP, LANE)

    def block(part, first):
        return jnp.concatenate([part(first), part(first + 1)], axis=1)

    blocks = [block(neighbour, tiles - 2)]
    blocks += [block(own, c) for c in range(0, tiles, 2)]
    blocks += [block(neighbour, 0)]
    shape = (HALF, HALF)
    from_here = (iota(shape, 0) >= iota(shape, 1)).astype(BF16)
    up_to_here = (iota(shape, 0) <= iota(shape, 1)).astype(BF16)
    band = jnp.concatenate([from_here, jnp.ones(shape, BF16), up_to_here], axis=0)
    count = COLS // HALF
    wide = jnp.concatenate(
        [jnp.concatenate(blocks[i : i + 3], axis=1) for i in range(count)], axis=0
    )
    box = sum(jnp.dot(t, band, preferred_element_type=F32) for t in split2(wide))
    for i in range(count):
        sums = box[i * GROUP : (i + 1) * GROUP]
        screen = sums[:OWN_DATES] / (1.0 + sums[OWN_DATES:SUMS])
        screens_ref[:, i * HALF : (i + 1) * HALF] = screen
        for c in range(i * HALF, (i + 1) * HALF, LANE):
            part = screen[:, c - i * HALF : c - i * HALF + LANE]
            for half in halves:
                rows = slice(half * SUB, (half + 1) * SUB)
                mask = mask_ref[rows, c : c + LANE].astype(F32)
                residual_ref[:, rows, c : c + LANE] = mask[None] * (
                    x_ref[half * tiles + c // LANE][:OWN_DATES] - part[:, None, :]
                )


def call(kernel, out_shape, in_specs, out_specs, scratch=(), flops=0, nbytes=0, vmem=VMEM_LIMIT):
    return pl.pallas_call(
        kernel,
        out_shape=out_shape,
        in_specs=in_specs,
        out_specs=out_specs,
        scratch_shapes=scratch,
        compiler_params=pltpu.CompilerParams(vmem_limit_bytes=vmem),
        cost_estimate=pl.CostEstimate(flops=flops, bytes_accessed=nbytes, transcendentals=0),
    )


def struct(*shape, dtype=F32):
    return jax.ShapeDtypeStruct(shape, dtype)


def body(phases, pairs, ref_pixel, coherent):
    send, cand = call(
        pack_kernel,
        (struct(STACK, OWN_IFGS, SUB, LANE), struct(1, LANE)),
        [full(pltpu.SMEM), full(pltpu.SMEM), full(pltpu.HBM)],
        (full(pltpu.HBM), full()),
        [
            pltpu.VMEM((OWN_IFGS, ROWS, COLS), F32),
            pltpu.SemaphoreType.DMA((FILLS,)),
            pltpu.SemaphoreType.DMA((FILLS, STACK)),
        ],
        nbytes=2 * 4 * OWN_IFGS * ROWS * COLS,
        vmem=BIG_LIMIT,
    )(ref_pixel, lax.axis_index(SPACE_AXES).reshape(1), phases)
    block = lax.all_to_all(send, STACK_AXES, split_axis=0, concat_axis=0, tiled=True)

    design, design_t, operator = call(
        operator_kernel,
        (
            struct(IFGS, 2 * DATES, dtype=BF16),
            struct(DATES, IFGS, dtype=BF16),
            struct(DATES + OUT_ROWS, 3 * DATES, dtype=BF16),
        ),
        [full()],
        (full(), full(), full()),
        flops=30 * 6 * 2 * 256**3,
        nbytes=10**6,
    )(pairs.T)

    refs = cand
    for axis in ("z_lo", "z_hi"):
        refs = jnp.sum(lax.all_gather(refs, axis, axis=0, tiled=True), axis=0, keepdims=True)
    refs, block, operator = lax.optimization_barrier((refs, block, operator))
    refs = lax.all_to_all(
        jnp.broadcast_to(refs, (2 * STACK, LANE)),
        ("x_hi",) + STACK_AXES,
        split_axis=0,
        concat_axis=0,
        tiled=True,
    )

    high, sums = call(
        invert_kernel,
        (struct(OUT_ROWS, PIXELS), struct(OUT_ROWS, LANE)),
        [full(pltpu.SMEM)] + [full()] * 6,
        (full(), full()),
        flops=6 * 2 * PIXELS * DATES * 1200,
        nbytes=4 * (IFGS + OUT_ROWS) * PIXELS,
    )(
        lax.axis_index(STACK_AXES).reshape(1),
        block.reshape(IFGS * SUB, LANE),
        refs,
        design,
        design_t,
        operator,
        coherent,
    )

    count = SPACE
    tiles = COLS // LANE
    edge = HALF // LANE
    moves = []
    for s in range(STACK):
        step = -1 if s % tiles < edge else 1 if s % tiles >= tiles - edge else 0
        moves += [
            (s * count + i, s * count + i + step)
            for i in range(count)
            if step and 0 <= i + step < count
        ]
    beside = lax.ppermute(sums, STACK_AXES + SPACE_AXES, moves)

    pieces = call(
        pieces_kernel,
        struct(STACK * PIECE * SUB, LANE),
        [full()] * 2,
        full(),
        nbytes=4 * 2 * STACK * PIECE * PIXELS,
    )(high, beside)
    dated = lax.all_to_all(
        pieces.reshape(STACK, PIECE, SUB, LANE), STACK_AXES, split_axis=0, concat_axis=0, tiled=True
    )

    return call(
        screen_kernel,
        (struct(OWN_DATES, COLS), struct(OWN_DATES, ROWS, COLS)),
        [full()] * 2,
        (full(), full()),
        flops=2 * 64 * 768 * 256 * 3,
        nbytes=2 * 4 * PIECE * ROWS * COLS,
    )(dated, coherent)


def solution(mesh):
    fine = Mesh(mesh.devices.reshape(4, 2, 2, 2, 4, 4), STACK_AXES + SPACE_AXES)
    return jax.shard_map(
        body,
        mesh=fine,
        in_specs=(P(STACK_AXES, None, SPACE_AXES), P(), P(), P(None, SPACE_AXES)),
        out_specs=(P(STACK_AXES, SPACE_AXES), P(STACK_AXES, None, SPACE_AXES)),
        check_vma=False,
    )
```

```python
import functools

import jax
import jax.numpy as jnp
from jax import lax
from jax.experimental import pallas as pl
from jax.experimental.pallas import tpu as pltpu
from jax.sharding import Mesh, PartitionSpec as P

IFGS = 576
DATES = 144
ROWS = 16
TAU = 8
HALF = 256
STACK = 16
OWN_IFGS = IFGS // STACK
OWN_DATES = DATES // STACK
COLS = 1024
SPACE = 32
SUB = 8
LANE = 128
GROUP = 16
OUT_ROWS = STACK * GROUP
SUMS = OWN_DATES + 1
PIECE = SUMS + GROUP // SUB
PIXELS = SUB * LANE
WIDE = 256

STACK_AXES = ("y", "x_lo", "core")
SPACE_AXES = ("x_hi", "z_hi", "z_lo")

F32 = jnp.float32
BF16 = jnp.bfloat16
HIGHEST = lax.Precision.HIGHEST
FILLS = 4
VMEM_LIMIT = 16 * 1024 * 1024
BIG_LIMIT = 56 * 1024 * 1024


def tile_of(piece):
    return (piece // 8) * SUB, (piece % 8) * LANE


def split2(value):
    first = value.astype(BF16)
    return first, (value - first.astype(F32)).astype(BF16)


def iota(shape, axis):
    return lax.broadcasted_iota(jnp.int32, shape, axis)


def full(memory_space=pltpu.VMEM):
    return pl.BlockSpec(memory_space=memory_space)


def pack_kernel(
    pixel_ref, space_ref, x_ref, out_ref, cand_ref, held, pieces, in_sems, out_sems
):
    step = OWN_IFGS // FILLS
    fills, sends = [], []
    for i in range(FILLS):
        ifgs = pl.ds(i * step, step)
        fills.append(
            pltpu.make_async_copy(x_ref.at[ifgs], held.at[ifgs], in_sems.at[i])
        )
        sends.append(
            pltpu.make_async_copy(pieces.at[i], out_ref.at[:, ifgs], out_sems.at[i])
        )
    fills[0].start()
    for i in range(FILLS):
        fills[i].wait()
        if i + 1 < FILLS:
            fills[i + 1].start()
        for piece in range(STACK):
            r, c = tile_of(piece)
            pieces[i, piece] = held[i * step : (i + 1) * step, r : r + SUB, c : c + LANE]
        sends[i].start()
    flat = pixel_ref[0]
    row = flat // (SPACE * COLS)
    col = lax.rem(flat, COLS)
    row_tile = pl.multiple_of((row // SUB) * SUB, SUB)
    col_tile = pl.multiple_of((col // LANE) * LANE, LANE)
    is_owner = space_ref[0] == lax.rem(flat, SPACE * COLS) // COLS
    picked = held[:, pl.ds(row_tile, SUB), pl.ds(col_tile, LANE)]
    shape = (OWN_IFGS, SUB, LANE)
    here = (iota(shape, 1) == lax.rem(row, SUB)) & (iota(shape, 2) == lax.rem(col, LANE))
    here = here & is_owner
    picked = jnp.sum(jnp.where(here, picked, 0.0), axis=1)
    picked = jnp.concatenate([picked, jnp.zeros((LANE - OWN_IFGS, LANE), F32)], axis=0)
    rows = lax.dot_general(
        jnp.ones((SUB, LANE), F32),
        picked,
        (((1,), (1,)), ((), ())),
        precision=HIGHEST,
        preferred_element_type=F32,
    )
    cand_ref[...] = rows[:1]
    for send in sends:
        send.wait()


def design_kernel(pairs_ref, design_t_ref):
    dates = iota((DATES, IFGS), 0)
    later = (pairs_ref[1:2, :] == dates).astype(F32)
    earlier = (pairs_ref[0:1, :] == dates).astype(F32)
    design_t = later - earlier
    design_t_ref[...] = design_t.astype(BF16)


def operator_kernel(design_t_ref, op_ref):
    normal = lax.dot_general(
        design_t_ref[...],
        design_t_ref[...],
        (((1,), (1,)), ((), ())),
        preferred_element_type=F32,
    )
    eye = (iota((DATES, DATES), 0) == iota((DATES, DATES), 1)).astype(F32)
    normal = normal + eye
    diag = jnp.sum(normal * eye, axis=0, keepdims=True)
    error = eye - normal / diag
    inverse = eye / diag
    bound = 7.0 * jnp.max(diag)
    mul = functools.partial(jnp.dot, precision=HIGHEST, preferred_element_type=F32)

    def step(carry):
        power, inv, err = carry
        return power * 2.0, inv + mul(inv, err), mul(err, err)

    _, inverse, _ = lax.while_loop(
        lambda carry: carry[0] < bound, step, (jnp.float32(1.0), inverse, error)
    )
    inverse = inverse + mul(inverse, eye - mul(normal, inverse))
    steps = iota((DATES, DATES), 0) - iota((DATES, DATES), 1)
    gauss = jnp.exp(-(steps * steps).astype(F32) / (2.0 * TAU * TAU))
    smooth = gauss / jnp.sum(gauss, axis=1, keepdims=True)
    high = mul(eye - smooth, inverse)
    out_row = iota((OUT_ROWS, DATES), 0)
    place = out_row & (GROUP - 1)
    date = jnp.where(place < OWN_DATES, (out_row >> 4) * OWN_DATES + place, -1)
    spread = (iota((OUT_ROWS, DATES), 1) == date).astype(F32)
    first, second = split2(jnp.concatenate([inverse, mul(spread, high)], axis=0))
    op_ref[...] = jnp.concatenate([first, second, first], axis=1)


def moment_kernel(x_ref, design_t_ref, moment_ref):
    dot = functools.partial(jnp.dot, preferred_element_type=F32)
    for first in range(0, SUB, WIDE // LANE):
        rows = range(first, first + WIDE // LANE)
        part = slice(first * LANE, first * LANE + WIDE)
        x = jnp.concatenate([x_ref[pl.ds(r, IFGS, stride=SUB), :] for r in rows], axis=1)
        moment_ref[:, part] = sum(dot(design_t_ref[...], term) for term in split2(x))


def invert_kernel(
    place_ref,
    x_ref,
    moment_ref,
    refs_ref,
    design_t_ref,
    op_ref,
    mask_ref,
    high_ref,
    sums_ref,
):
    place = place_ref[0]
    row_tile = pl.multiple_of((place // 8) * SUB, SUB)
    col_tile = pl.multiple_of(lax.rem(place, 8) * LANE, LANE)
    coherent = mask_ref[pl.ds(row_tile, SUB), pl.ds(col_tile, LANE)].astype(F32)
    is_weight = (iota((OUT_ROWS, LANE), 0) & (GROUP - 1)) == OWN_DATES
    ifg = iota((IFGS, STACK), 0)
    spread = (iota((IFGS, STACK), 1) == (ifg * 1821) >> 16).astype(F32)
    refs = refs_ref[:STACK] + refs_ref[STACK:]
    refs = jnp.dot(spread, refs, precision=HIGHEST, preferred_element_type=F32)
    ifg = iota((IFGS, LANE), 0)
    own = iota((IFGS, LANE), 1) == ifg - ((ifg * 1821) >> 16) * OWN_IFGS
    ref_phase = jnp.sum(jnp.where(own, refs, 0.0), axis=1, keepdims=True)
    dot = functools.partial(jnp.dot, preferred_element_type=F32)
    design = design_t_ref[...].astype(F32).T
    design = jnp.concatenate([design, design], axis=1).astype(BF16)
    ref_columns = jnp.broadcast_to(ref_phase, (IFGS, LANE))
    ref_moment = sum(dot(design_t_ref[...], term) for term in split2(ref_columns))
    ref_moment = jnp.concatenate([ref_moment] * (WIDE // LANE), axis=1)
    sums = jnp.zeros((OUT_ROWS, LANE), F32)
    for first in range(0, SUB, WIDE // LANE):
        rows = range(first, first + WIDE // LANE)
        columns = slice(first * LANE, first * LANE + WIDE)
        x = jnp.concatenate([x_ref[pl.ds(r, IFGS, stride=SUB), :] for r in rows], axis=1)
        x = x - ref_phase
        moment, moment_rest = split2(moment_ref[:, columns] - ref_moment)
        both = dot(op_ref[...], jnp.concatenate([moment, moment, moment_rest], axis=0))
        model = dot(design, jnp.concatenate(split2(both[:DATES]), axis=0))
        gap = x - model
        misfit = jnp.sum(gap * gap, axis=0, keepdims=True) * (1.0 / IFGS)
        for i, r in enumerate(rows):
            part = slice(i * LANE, (i + 1) * LANE)
            weight = coherent[r : r + 1] / (1.0 + misfit[:, part])
            high = jnp.where(is_weight, 1.0, both[DATES:, part])
            weighted = high * weight
            sums = sums + weighted
            high = jnp.where(is_weight, weighted, high)
            high_ref[:, r * LANE : (r + 1) * LANE] = high
    sums_ref[...] = sums


def pieces_kernel(high_ref, sums_ref, out_ref):
    for r in range(SUB):
        for t in range(STACK):
            out_ref[pl.ds(t * PIECE * SUB + r, SUMS, stride=SUB), :] = high_ref[
                t * GROUP : t * GROUP + SUMS, r * LANE : (r + 1) * LANE
            ]
    for t in range(STACK):
        last = t * PIECE * SUB + SUMS * SUB
        out_ref[last : last + GROUP] = sums_ref[t * GROUP : (t + 1) * GROUP]


def screen_kernel(x_ref, mask_ref, screens_ref, residual_ref):
    halves = range(ROWS // SUB)
    tiles = COLS // LANE

    def own(c):
        total = 0.0
        for half in halves:
            piece = x_ref[half * tiles + c]
            weight = piece[OWN_DATES:SUMS]
            part = jnp.concatenate([piece[:OWN_DATES] * weight, weight], axis=0)
            total = total + part
        total = jnp.sum(total, axis=1)
        return jnp.concatenate([total, jnp.zeros((GROUP - SUMS, LANE), F32)], axis=0)

    def neighbour(c):
        total = sum(x_ref[half * tiles + c, SUMS:] for half in halves)
        return total.reshape(GROUP, LANE)

    def block(part, first):
        return jnp.concatenate([part(first), part(first + 1)], axis=1)

    blocks = [block(neighbour, tiles - 2)]
    blocks += [block(own, c) for c in range(0, tiles, 2)]
    blocks += [block(neighbour, 0)]
    shape = (HALF, HALF)
    from_here = (iota(shape, 0) >= iota(shape, 1)).astype(BF16)
    up_to_here = (iota(shape, 0) <= iota(shape, 1)).astype(BF16)
    band = jnp.concatenate([from_here, jnp.ones(shape, BF16), up_to_here], axis=0)
    count = COLS // HALF
    wide = jnp.concatenate(
        [jnp.concatenate(blocks[i : i + 3], axis=1) for i in range(count)], axis=0
    )
    box = sum(jnp.dot(t, band, preferred_element_type=F32) for t in split2(wide))
    for i in range(count):
        sums = box[i * GROUP : (i + 1) * GROUP]
        screen = sums[:OWN_DATES] / (1.0 + sums[OWN_DATES:SUMS])
        screens_ref[:, i * HALF : (i + 1) * HALF] = screen
        for c in range(i * HALF, (i + 1) * HALF, LANE):
            part = screen[:, c - i * HALF : c - i * HALF + LANE]
            for half in halves:
                rows = slice(half * SUB, (half + 1) * SUB)
                mask = mask_ref[rows, c : c + LANE].astype(F32)
                residual_ref[:, rows, c : c + LANE] = mask[None] * (
                    x_ref[half * tiles + c // LANE][:OWN_DATES] - part[:, None, :]
                )


def call(kernel, out_shape, in_specs, out_specs, scratch=(), flops=0, nbytes=0, vmem=VMEM_LIMIT):
    return pl.pallas_call(
        kernel,
        out_shape=out_shape,
        in_specs=in_specs,
        out_specs=out_specs,
        scratch_shapes=scratch,
        compiler_params=pltpu.CompilerParams(vmem_limit_bytes=vmem),
        cost_estimate=pl.CostEstimate(flops=flops, bytes_accessed=nbytes, transcendentals=0),
    )


def struct(*shape, dtype=F32):
    return jax.ShapeDtypeStruct(shape, dtype)


def body(phases, pairs, ref_pixel, coherent):
    send, cand = call(
        pack_kernel,
        (struct(STACK, OWN_IFGS, SUB, LANE), struct(1, LANE)),
        [full(pltpu.SMEM), full(pltpu.SMEM), full(pltpu.HBM)],
        (full(pltpu.HBM), full()),
        [
            pltpu.VMEM((OWN_IFGS, ROWS, COLS), F32),
            pltpu.VMEM((FILLS, STACK, OWN_IFGS // FILLS, SUB, LANE), F32),
            pltpu.SemaphoreType.DMA((FILLS,)),
            pltpu.SemaphoreType.DMA((FILLS,)),
        ],
        nbytes=2 * 4 * OWN_IFGS * ROWS * COLS,
        vmem=BIG_LIMIT,
    )(ref_pixel, lax.axis_index(SPACE_AXES).reshape(1), phases)
    block = lax.all_to_all(send, STACK_AXES, split_axis=0, concat_axis=0, tiled=True)

    design_t = call(
        design_kernel,
        struct(DATES, IFGS, dtype=BF16),
        [full()],
        full(),
        flops=10**4,
        nbytes=10**4,
    )(pairs.T)

    refs = cand
    for axis in ("z_lo", "z_hi"):
        refs = jnp.sum(lax.all_gather(refs, axis, axis=0, tiled=True), axis=0, keepdims=True)
    refs = jnp.broadcast_to(refs, (2 * STACK, LANE))
    refs, block, design_t = lax.optimization_barrier((refs, block, design_t))
    refs = lax.all_to_all(
        refs, ("x_hi",) + STACK_AXES, split_axis=0, concat_axis=0, tiled=True
    )

    operator = call(
        operator_kernel,
        struct(DATES + OUT_ROWS, 3 * DATES, dtype=BF16),
        [full()],
        full(),
        flops=10**4,
        nbytes=10**4,
    )(design_t)

    flat = block.reshape(IFGS * SUB, LANE)
    moment = call(
        moment_kernel,
        struct(DATES, PIXELS),
        [full()] * 2,
        full(),
        flops=10**4,
        nbytes=10**4,
    )(flat, design_t)

    high, sums = call(
        invert_kernel,
        (struct(OUT_ROWS, PIXELS), struct(OUT_ROWS, LANE)),
        [full(pltpu.SMEM)] + [full()] * 6,
        (full(), full()),
        flops=6 * 2 * PIXELS * DATES * 1200,
        nbytes=4 * (IFGS + OUT_ROWS) * PIXELS,
    )(
        lax.axis_index(STACK_AXES).reshape(1),
        flat,
        moment,
        refs,
        design_t,
        operator,
        coherent,
    )

    count = SPACE
    tiles = COLS // LANE
    edge = HALF // LANE
    moves = []
    for s in range(STACK):
        step = -1 if s % tiles < edge else 1 if s % tiles >= tiles - edge else 0
        moves += [
            (s * count + i, s * count + i + step)
            for i in range(count)
            if step and 0 <= i + step < count
        ]
    beside = lax.ppermute(sums, STACK_AXES + SPACE_AXES, moves)

    pieces = call(
        pieces_kernel,
        struct(STACK * PIECE * SUB, LANE),
        [full()] * 2,
        full(),
        nbytes=4 * 2 * STACK * PIECE * PIXELS,
    )(high, beside)
    dated = lax.all_to_all(
        pieces.reshape(STACK, PIECE, SUB, LANE), STACK_AXES, split_axis=0, concat_axis=0, tiled=True
    )

    return call(
        screen_kernel,
        (struct(OWN_DATES, COLS), struct(OWN_DATES, ROWS, COLS)),
        [full()] * 2,
        (full(), full()),
        flops=2 * 64 * 768 * 256 * 3,
        nbytes=2 * 4 * PIECE * ROWS * COLS,
    )(dated, coherent)


def solution(mesh):
    fine = Mesh(mesh.devices.reshape(4, 2, 2, 2, 4, 4), STACK_AXES + SPACE_AXES)
    return jax.shard_map(
        body,
        mesh=fine,
        in_specs=(P(STACK_AXES, None, SPACE_AXES), P(), P(), P(None, SPACE_AXES)),
        out_specs=(P(STACK_AXES, SPACE_AXES), P(STACK_AXES, None, SPACE_AXES)),
        check_vma=False,
    )
```

```python
import functools

import jax
import jax.numpy as jnp
from jax import lax
from jax.experimental import pallas as pl
from jax.experimental.pallas import tpu as pltpu
from jax.sharding import Mesh, PartitionSpec as P

IFGS = 576
DATES = 144
ROWS = 16
TAU = 8
HALF = 256
STACK = 16
OWN_IFGS = IFGS // STACK
OWN_DATES = DATES // STACK
COLS = 1024
SPACE = 32
SUB = 8
LANE = 128
GROUP = 16
OUT_ROWS = STACK * GROUP
SUMS = OWN_DATES + 1
PIECE = SUMS + GROUP // SUB
PIXELS = SUB * LANE
WIDE = 512

STACK_AXES = ("y", "x_lo", "core")
SPACE_AXES = ("x_hi", "z_hi", "z_lo")

F32 = jnp.float32
BF16 = jnp.bfloat16
HIGHEST = lax.Precision.HIGHEST
VMEM_LIMIT = 24 * 1024 * 1024
BIG_LIMIT = 60 * 1024 * 1024


def tile_of(piece):
    return (piece // 8) * SUB, (piece % 8) * LANE


def split2(value):
    first = value.astype(BF16)
    return first, (value - first.astype(F32)).astype(BF16)


def split3(value):
    first, rest = split2(value)
    third = value - first.astype(F32) - rest.astype(F32)
    return first, rest, third.astype(BF16)


def iota(shape, axis):
    return lax.broadcasted_iota(jnp.int32, shape, axis)


def full(memory_space=pltpu.VMEM):
    return pl.BlockSpec(memory_space=memory_space)


def pack_kernel(pixel_ref, space_ref, x_ref, out_ref, cand_ref, held, in_sems, out_sems):
    fills, sends = [], []
    for piece in range(STACK):
        r, c = tile_of(piece)
        fills.append(
            pltpu.make_async_copy(
                x_ref.at[:, pl.ds(r, SUB), pl.ds(c, LANE)], held.at[piece], in_sems.at[piece]
            )
        )
        sends.append(
            pltpu.make_async_copy(held.at[piece], out_ref.at[piece], out_sems.at[piece])
        )
        fills[-1].start()
    for fill, send in zip(fills, sends):
        fill.wait()
        send.start()
    flat = pixel_ref[0]
    row = flat // (SPACE * COLS)
    col = lax.rem(flat, COLS)
    is_owner = space_ref[0] == lax.rem(flat, SPACE * COLS) // COLS
    picked = held[(row // SUB) * (COLS // LANE) + col // LANE]
    shape = (OWN_IFGS, SUB, LANE)
    here = (iota(shape, 1) == lax.rem(row, SUB)) & (iota(shape, 2) == lax.rem(col, LANE))
    here = here & is_owner
    picked = jnp.sum(jnp.where(here, picked, 0.0), axis=1)
    picked = jnp.concatenate([picked, jnp.zeros((LANE - OWN_IFGS, LANE), F32)], axis=0)
    rows = lax.dot_general(
        jnp.ones((SUB, LANE), F32),
        picked,
        (((1,), (1,)), ((), ())),
        precision=HIGHEST,
        preferred_element_type=F32,
    )
    cand_ref[...] = rows[:1]
    for send in sends:
        send.wait()


def rows_kernel(parts_ref, rows_ref):
    total = jnp.sum(parts_ref[...], axis=0, keepdims=True)
    rows_ref[...] = jnp.broadcast_to(total, rows_ref.shape)


def operator_kernel(pairs_ref, design_ref, design_t_ref, op_ref):
    dates = iota((DATES, IFGS), 0)
    later = (pairs_ref[1:2, :] == dates).astype(F32)
    earlier = (pairs_ref[0:1, :] == dates).astype(F32)
    design_t = later - earlier
    design_t_ref[...] = design_t.astype(BF16)
    design_ref[...] = jnp.concatenate([design_t.T] * 2, axis=1).astype(BF16)
    normal = lax.dot_general(
        design_t.astype(BF16),
        design_t.astype(BF16),
        (((1,), (1,)), ((), ())),
        preferred_element_type=F32,
    )
    eye = (iota((DATES, DATES), 0) == iota((DATES, DATES), 1)).astype(F32)
    normal = normal + eye
    diag = jnp.sum(normal * eye, axis=0, keepdims=True)
    error = eye - normal / diag
    inverse = eye / diag
    bound = 7.0 * jnp.max(diag)
    mul = functools.partial(jnp.dot, precision=HIGHEST, preferred_element_type=F32)

    def step(carry):
        power, inv, err = carry
        return power * 2.0, inv + mul(inv, err), mul(err, err)

    _, inverse, _ = lax.while_loop(
        lambda carry: carry[0] < bound, step, (jnp.float32(1.0), inverse, error)
    )
    inverse = inverse + mul(inverse, eye - mul(normal, inverse))
    out_row = iota((OUT_ROWS, DATES), 0)
    place = out_row & (GROUP - 1)
    date = (out_row >> 4) * OWN_DATES + place
    steps = date - iota((OUT_ROWS, DATES), 1)
    gauss = jnp.exp(-(steps * steps).astype(F32) / (2.0 * TAU * TAU))
    smooth = gauss / jnp.sum(gauss, axis=1, keepdims=True)
    keep = (steps == 0).astype(F32) - smooth
    high = mul(jnp.where(place < OWN_DATES, keep, 0.0), inverse)
    first, second = split2(jnp.concatenate([inverse, high], axis=0))
    op_ref[...] = jnp.concatenate([first, second, first], axis=1)


def invert_kernel(
    place_ref, x_ref, refs_ref, design_ref, design_t_ref, op_ref, mask_ref, high_ref, sums_ref
):
    place = place_ref[0]
    row_tile = pl.multiple_of((place // 8) * SUB, SUB)
    col_tile = pl.multiple_of(lax.rem(place, 8) * LANE, LANE)
    coherent = mask_ref[pl.ds(row_tile, SUB), pl.ds(col_tile, LANE)].astype(F32)
    is_weight = (iota((OUT_ROWS, LANE), 0) & (GROUP - 1)) == OWN_DATES
    ifg = iota((IFGS, STACK), 0)
    spread = (iota((IFGS, STACK), 1) == (ifg * 1821) >> 16).astype(F32)
    spread = jnp.concatenate([spread] * 3, axis=1).astype(BF16)
    refs = refs_ref[:STACK] + refs_ref[STACK:]
    refs = jnp.dot(
        spread, jnp.concatenate(split3(refs), axis=0), preferred_element_type=F32
    )
    ifg = iota((IFGS, LANE), 0)
    own = iota((IFGS, LANE), 1) == ifg - ((ifg * 1821) >> 16) * OWN_IFGS
    ref_phase = jnp.sum(jnp.where(own, refs, 0.0), axis=1, keepdims=True)
    rows_at_once = WIDE // LANE
    dot = functools.partial(jnp.dot, preferred_element_type=F32)
    sums = jnp.zeros((OUT_ROWS, LANE), F32)
    for first in range(0, SUB, rows_at_once):
        rows = range(first, first + rows_at_once)
        x = jnp.concatenate([x_ref[pl.ds(r, IFGS, stride=SUB), :] for r in rows], axis=1)
        x = x - ref_phase
        moment, moment_rest = split2(sum(dot(design_t_ref[...], term) for term in split2(x)))
        both = dot(op_ref[...], jnp.concatenate([moment, moment, moment_rest], axis=0))
        model = dot(design_ref[...], jnp.concatenate(split2(both[:DATES]), axis=0))
        gap = x - model
        misfit = jnp.sum(gap * gap, axis=0, keepdims=True) * (1.0 / IFGS)
        for i, r in enumerate(rows):
            part = slice(i * LANE, (i + 1) * LANE)
            weight = coherent[r : r + 1] / (1.0 + misfit[:, part])
            high = jnp.where(is_weight, 1.0, both[DATES:, part])
            weighted = high * weight
            sums = sums + weighted
            high = jnp.where(is_weight, weighted, high)
            high_ref[:, r * LANE : (r + 1) * LANE] = high
    for t in range(STACK):
        sums_ref[t * SUMS : (t + 1) * SUMS] = sums[t * GROUP : t * GROUP + SUMS]


def pieces_kernel(high_ref, sums_ref, out_ref):
    for r in range(SUB):
        for t in range(STACK):
            out_ref[pl.ds(t * PIECE * SUB + r, SUMS, stride=SUB), :] = high_ref[
                t * GROUP : t * GROUP + SUMS, r * LANE : (r + 1) * LANE
            ]
    for t in range(STACK):
        last = t * PIECE * SUB + SUMS * SUB
        sums = sums_ref[t * SUMS : (t + 1) * SUMS]
        pad = jnp.zeros((GROUP - SUMS, LANE), F32)
        out_ref[last : last + GROUP] = jnp.concatenate([sums, pad], axis=0)


def screen_kernel(x_ref, mask_ref, screens_ref, residual_ref):
    halves = range(ROWS // SUB)
    tiles = COLS // LANE

    def own(c):
        total = 0.0
        for half in halves:
            piece = x_ref[half * tiles + c]
            weight = piece[OWN_DATES:SUMS]
            part = jnp.concatenate([piece[:OWN_DATES] * weight, weight], axis=0)
            total = total + part
        total = jnp.sum(total, axis=1)
        return jnp.concatenate([total, jnp.zeros((GROUP - SUMS, LANE), F32)], axis=0)

    def neighbour(c):
        total = sum(x_ref[half * tiles + c, SUMS:] for half in halves)
        return total.reshape(GROUP, LANE)

    def block(part, first):
        return jnp.concatenate([part(first), part(first + 1)], axis=1)

    blocks = [block(neighbour, tiles - 2)]
    blocks += [block(own, c) for c in range(0, tiles, 2)]
    blocks += [block(neighbour, 0)]
    shape = (HALF, HALF)
    from_here = (iota(shape, 0) >= iota(shape, 1)).astype(BF16)
    up_to_here = (iota(shape, 0) <= iota(shape, 1)).astype(BF16)
    band = jnp.concatenate([from_here, jnp.ones(shape, BF16), up_to_here], axis=0)
    count = COLS // HALF
    wide = jnp.concatenate(
        [jnp.concatenate(blocks[i : i + 3], axis=1) for i in range(count)], axis=0
    )
    box = sum(jnp.dot(t, band, preferred_element_type=F32) for t in split2(wide))
    for i in range(count):
        sums = box[i * GROUP : (i + 1) * GROUP]
        screen = sums[:OWN_DATES] / (1.0 + sums[OWN_DATES:SUMS])
        screens_ref[:, i * HALF : (i + 1) * HALF] = screen
        for c in range(i * HALF, (i + 1) * HALF, LANE):
            part = screen[:, c - i * HALF : c - i * HALF + LANE]
            for half in halves:
                rows = slice(half * SUB, (half + 1) * SUB)
                mask = mask_ref[rows, c : c + LANE].astype(F32)
                residual_ref[:, rows, c : c + LANE] = mask[None] * (
                    x_ref[half * tiles + c // LANE][:OWN_DATES] - part[:, None, :]
                )


def call(kernel, out_shape, in_specs, out_specs, scratch=(), flops=0, nbytes=0, vmem=VMEM_LIMIT):
    return pl.pallas_call(
        kernel,
        out_shape=out_shape,
        in_specs=in_specs,
        out_specs=out_specs,
        scratch_shapes=scratch,
        compiler_params=pltpu.CompilerParams(vmem_limit_bytes=vmem),
        cost_estimate=pl.CostEstimate(flops=flops, bytes_accessed=nbytes, transcendentals=0),
    )


def struct(*shape, dtype=F32):
    return jax.ShapeDtypeStruct(shape, dtype)


def body(phases, pairs, ref_pixel, coherent):
    send, cand = call(
        pack_kernel,
        (struct(STACK, OWN_IFGS, SUB, LANE), struct(1, LANE)),
        [full(pltpu.SMEM), full(pltpu.SMEM), full(pltpu.HBM)],
        (full(pltpu.HBM), full()),
        [
            pltpu.VMEM((STACK, OWN_IFGS, SUB, LANE), F32),
            pltpu.SemaphoreType.DMA((STACK,)),
            pltpu.SemaphoreType.DMA((STACK,)),
        ],
        nbytes=2 * 4 * OWN_IFGS * ROWS * COLS,
        vmem=BIG_LIMIT,
    )(ref_pixel, lax.axis_index(SPACE_AXES).reshape(1), phases)
    block = lax.all_to_all(send, STACK_AXES, split_axis=0, concat_axis=0, tiled=True)

    design, design_t, operator = call(
        operator_kernel,
        (
            struct(IFGS, 2 * DATES, dtype=BF16),
            struct(DATES, IFGS, dtype=BF16),
            struct(DATES + OUT_ROWS, 3 * DATES, dtype=BF16),
        ),
        [full()],
        (full(), full(), full()),
        flops=30 * 6 * 2 * 256**3,
        nbytes=10**6,
    )(pairs.T)

    refs = lax.all_gather(cand, "z_lo", axis=0, tiled=True)
    refs = jnp.sum(refs, axis=0, keepdims=True)
    refs = lax.all_gather(refs, "z_hi", axis=0, tiled=True)
    refs = call(rows_kernel, struct(2 * STACK, LANE), [full()], full())(refs)
    refs, block, operator = lax.optimization_barrier((refs, block, operator))
    refs = lax.all_to_all(
        refs,
        ("x_hi",) + STACK_AXES,
        split_axis=0,
        concat_axis=0,
        tiled=True,
    )

    high, sums = call(
        invert_kernel,
        (struct(OUT_ROWS, PIXELS), struct(STACK * SUMS, LANE)),
        [full(pltpu.SMEM)] + [full()] * 6,
        (full(), full()),
        flops=6 * 2 * PIXELS * DATES * 1200,
        nbytes=4 * (IFGS + OUT_ROWS) * PIXELS,
    )(
        lax.axis_index(STACK_AXES).reshape(1),
        block.reshape(IFGS * SUB, LANE),
        refs,
        design,
        design_t,
        operator,
        coherent,
    )

    count = SPACE
    tiles = COLS // LANE
    edge = HALF // LANE
    moves = []
    for s in range(STACK):
        step = -1 if s % tiles < edge else 1 if s % tiles >= tiles - edge else 0
        moves += [
            (s * count + i, s * count + i + step)
            for i in range(count)
            if step and 0 <= i + step < count
        ]
    beside = lax.ppermute(sums, STACK_AXES + SPACE_AXES, moves)

    pieces = call(
        pieces_kernel,
        struct(STACK * PIECE * SUB, LANE),
        [full()] * 2,
        full(),
        nbytes=4 * 2 * STACK * PIECE * PIXELS,
    )(high, beside)
    dated = lax.all_to_all(
        pieces.reshape(STACK, PIECE, SUB, LANE), STACK_AXES, split_axis=0, concat_axis=0, tiled=True
    )

    return call(
        screen_kernel,
        (struct(OWN_DATES, COLS), struct(OWN_DATES, ROWS, COLS)),
        [full()] * 2,
        (full(), full()),
        flops=2 * 64 * 768 * 256 * 3,
        nbytes=2 * 4 * PIECE * ROWS * COLS,
    )(dated, coherent)


def solution(mesh):
    fine = Mesh(mesh.devices.reshape(4, 2, 2, 2, 4, 4), STACK_AXES + SPACE_AXES)
    return jax.shard_map(
        body,
        mesh=fine,
        in_specs=(P(STACK_AXES, None, SPACE_AXES), P(), P(), P(None, SPACE_AXES)),
        out_specs=(P(STACK_AXES, SPACE_AXES), P(STACK_AXES, None, SPACE_AXES)),
        check_vma=False,
    )
```

```python
import functools

import jax
import jax.numpy as jnp
from jax import lax
from jax.experimental import pallas as pl
from jax.experimental.pallas import tpu as pltpu
from jax.sharding import Mesh, PartitionSpec as P

IFGS = 576
DATES = 144
ROWS = 16
TAU = 8
HALF = 256
STACK = 16
OWN_IFGS = IFGS // STACK
OWN_DATES = DATES // STACK
COLS = 1024
SPACE = 32
SUB = 8
LANE = 128
GROUP = 16
OUT_ROWS = STACK * GROUP
SUMS = OWN_DATES + 1
PIECE = SUMS + GROUP // SUB
PIXELS = SUB * LANE
WIDE = 512

STACK_AXES = ("y", "x_lo", "core")
SPACE_AXES = ("x_hi", "z_hi", "z_lo")

F32 = jnp.float32
BF16 = jnp.bfloat16
HIGHEST = lax.Precision.HIGHEST
VMEM_LIMIT = 24 * 1024 * 1024
BIG_LIMIT = 60 * 1024 * 1024


def tile_of(piece):
    return (piece // 8) * SUB, (piece % 8) * LANE


def split2(value):
    first = value.astype(BF16)
    return first, (value - first.astype(F32)).astype(BF16)


def split3(value):
    first, rest = split2(value)
    third = value - first.astype(F32) - rest.astype(F32)
    return first, rest, third.astype(BF16)


def iota(shape, axis):
    return lax.broadcasted_iota(jnp.int32, shape, axis)


def full(memory_space=pltpu.VMEM):
    return pl.BlockSpec(memory_space=memory_space)


def pack_kernel(pixel_ref, space_ref, x_ref, out_ref, cand_ref, held, in_sems, out_sems):
    fills, sends = [], []
    for piece in range(STACK):
        r, c = tile_of(piece)
        fills.append(
            pltpu.make_async_copy(
                x_ref.at[:, pl.ds(r, SUB), pl.ds(c, LANE)], held.at[piece], in_sems.at[piece]
            )
        )
        sends.append(
            pltpu.make_async_copy(held.at[piece], out_ref.at[piece], out_sems.at[piece])
        )
        fills[-1].start()
    for fill, send in zip(fills, sends):
        fill.wait()
        send.start()
    flat = pixel_ref[0]
    row = flat // (SPACE * COLS)
    col = lax.rem(flat, COLS)
    is_owner = space_ref[0] == lax.rem(flat, SPACE * COLS) // COLS
    picked = held[(row // SUB) * (COLS // LANE) + col // LANE]
    shape = (OWN_IFGS, SUB, LANE)
    here = (iota(shape, 1) == lax.rem(row, SUB)) & (iota(shape, 2) == lax.rem(col, LANE))
    here = here & is_owner
    picked = jnp.sum(jnp.where(here, picked, 0.0), axis=1)
    picked = jnp.concatenate([picked, jnp.zeros((LANE - OWN_IFGS, LANE), F32)], axis=0)
    rows = lax.dot_general(
        jnp.ones((SUB, LANE), F32),
        picked,
        (((1,), (1,)), ((), ())),
        precision=HIGHEST,
        preferred_element_type=F32,
    )
    cand_ref[...] = rows[:1]
    for send in sends:
        send.wait()


def rows_kernel(parts_ref, rows_ref):
    total = jnp.sum(parts_ref[...], axis=0, keepdims=True)
    rows_ref[...] = jnp.broadcast_to(total, rows_ref.shape)


def design_kernel(pairs_ref, design_t_ref):
    dates = iota((DATES, IFGS), 0)
    later = (pairs_ref[1:2, :] == dates).astype(F32)
    earlier = (pairs_ref[0:1, :] == dates).astype(F32)
    design_t = later - earlier
    design_t_ref[...] = design_t.astype(BF16)


def operator_kernel(design_t_ref, op_ref):
    design = design_t_ref[...].astype(F32).T
    design = jnp.concatenate([design, design, jnp.zeros_like(design)], axis=1)
    op_ref[DATES + OUT_ROWS :] = design.astype(BF16)
    design_t = design_t_ref[...]
    normal = lax.dot_general(
        design_t,
        design_t,
        (((1,), (1,)), ((), ())),
        preferred_element_type=F32,
    )
    eye = (iota((DATES, DATES), 0) == iota((DATES, DATES), 1)).astype(F32)
    normal = normal + eye
    diag = jnp.sum(normal * eye, axis=0, keepdims=True)
    error = eye - normal / diag
    inverse = eye / diag
    bound = 7.0 * jnp.max(diag)
    mul = functools.partial(jnp.dot, precision=HIGHEST, preferred_element_type=F32)

    def step(carry):
        power, inv, err = carry
        return power * 2.0, inv + mul(inv, err), mul(err, err)

    _, inverse, _ = lax.while_loop(
        lambda carry: carry[0] < bound, step, (jnp.float32(1.0), inverse, error)
    )
    inverse = inverse + mul(inverse, eye - mul(normal, inverse))
    out_row = iota((OUT_ROWS, DATES), 0)
    place = out_row & (GROUP - 1)
    date = (out_row >> 4) * OWN_DATES + place
    steps = date - iota((OUT_ROWS, DATES), 1)
    gauss = jnp.exp(-(steps * steps).astype(F32) / (2.0 * TAU * TAU))
    smooth = gauss / jnp.sum(gauss, axis=1, keepdims=True)
    keep = (steps == 0).astype(F32) - smooth
    high = mul(jnp.where(place < OWN_DATES, keep, 0.0), inverse)
    first, second = split2(jnp.concatenate([inverse, high], axis=0))
    op_ref[: DATES + OUT_ROWS] = jnp.concatenate([first, second, first], axis=1)


def mask_kernel(place_ref, mask_ref, tile_ref):
    place = place_ref[0]
    row_tile = pl.multiple_of((place // 8) * SUB, SUB)
    col_tile = pl.multiple_of(lax.rem(place, 8) * LANE, LANE)
    tile_ref[...] = mask_ref[pl.ds(row_tile, SUB), pl.ds(col_tile, LANE)].astype(F32)


def invert_kernel(
    x_ref, refs_ref, design_t_ref, op_ref, mask_ref, high_ref, sums_ref
):
    coherent = mask_ref[...]
    is_weight = (iota((OUT_ROWS, LANE), 0) & (GROUP - 1)) == OWN_DATES
    ifg = iota((IFGS, STACK), 0)
    spread = (iota((IFGS, STACK), 1) == (ifg * 1821) >> 16).astype(F32)
    spread = jnp.concatenate([spread] * 3, axis=1).astype(BF16)
    refs = refs_ref[...]
    refs = jnp.dot(
        spread, jnp.concatenate(split3(refs), axis=0), preferred_element_type=F32
    )
    ifg = iota((IFGS, LANE), 0)
    own = iota((IFGS, LANE), 1) == ifg - ((ifg * 1821) >> 16) * OWN_IFGS
    ref_phase = jnp.sum(jnp.where(own, refs, 0.0), axis=1, keepdims=True)
    rows_at_once = WIDE // LANE
    dot = functools.partial(jnp.dot, preferred_element_type=F32)
    design = op_ref[DATES + OUT_ROWS :, : 2 * DATES]
    sums = jnp.zeros((OUT_ROWS, LANE), F32)
    for first in range(0, SUB, rows_at_once):
        rows = range(first, first + rows_at_once)
        x = jnp.concatenate([x_ref[pl.ds(r, IFGS, stride=SUB), :] for r in rows], axis=1)
        x = x - ref_phase
        moment, moment_rest = split2(sum(dot(design_t_ref[...], term) for term in split2(x)))
        both = dot(
            op_ref[: DATES + OUT_ROWS], jnp.concatenate([moment, moment, moment_rest], axis=0)
        )
        model = dot(design, jnp.concatenate(split2(both[:DATES]), axis=0))
        gap = x - model
        misfit = jnp.sum(gap * gap, axis=0, keepdims=True) * (1.0 / IFGS)
        for i, r in enumerate(rows):
            part = slice(i * LANE, (i + 1) * LANE)
            weight = coherent[r : r + 1] / (1.0 + misfit[:, part])
            high = jnp.where(is_weight, 1.0, both[DATES:, part])
            weighted = high * weight
            sums = sums + weighted
            high = jnp.where(is_weight, weighted, high)
            high_ref[:, r * LANE : (r + 1) * LANE] = high
    for t in range(STACK):
        sums_ref[t * SUMS : (t + 1) * SUMS] = sums[t * GROUP : t * GROUP + SUMS]


def pieces_kernel(high_ref, sums_ref, out_ref):
    for r in range(SUB):
        for t in range(STACK):
            out_ref[pl.ds(t * PIECE * SUB + r, SUMS, stride=SUB), :] = high_ref[
                t * GROUP : t * GROUP + SUMS, r * LANE : (r + 1) * LANE
            ]
    for t in range(STACK):
        last = t * PIECE * SUB + SUMS * SUB
        sums = sums_ref[t * SUMS : (t + 1) * SUMS]
        pad = jnp.zeros((GROUP - SUMS, LANE), F32)
        out_ref[last : last + GROUP] = jnp.concatenate([sums, pad], axis=0)


def screen_kernel(x_ref, mask_ref, screens_ref, residual_ref):
    halves = range(ROWS // SUB)
    tiles = COLS // LANE

    def own(c):
        total = 0.0
        for half in halves:
            piece = x_ref[half * tiles + c]
            weight = piece[OWN_DATES:SUMS]
            part = jnp.concatenate([piece[:OWN_DATES] * weight, weight], axis=0)
            total = total + part
        total = jnp.sum(total, axis=1)
        return jnp.concatenate([total, jnp.zeros((GROUP - SUMS, LANE), F32)], axis=0)

    def neighbour(c):
        total = sum(x_ref[half * tiles + c, SUMS:] for half in halves)
        return total.reshape(GROUP, LANE)

    def block(part, first):
        return jnp.concatenate([part(first), part(first + 1)], axis=1)

    blocks = [block(neighbour, tiles - 2)]
    blocks += [block(own, c) for c in range(0, tiles, 2)]
    blocks += [block(neighbour, 0)]
    shape = (HALF, HALF)
    from_here = (iota(shape, 0) >= iota(shape, 1)).astype(BF16)
    up_to_here = (iota(shape, 0) <= iota(shape, 1)).astype(BF16)
    band = jnp.concatenate([from_here, jnp.ones(shape, BF16), up_to_here], axis=0)
    count = COLS // HALF
    wide = jnp.concatenate(
        [jnp.concatenate(blocks[i : i + 3], axis=1) for i in range(count)], axis=0
    )
    box = sum(jnp.dot(t, band, preferred_element_type=F32) for t in split2(wide))
    for i in range(count):
        sums = box[i * GROUP : (i + 1) * GROUP]
        screen = sums[:OWN_DATES] / (1.0 + sums[OWN_DATES:SUMS])
        screens_ref[:, i * HALF : (i + 1) * HALF] = screen
        for c in range(i * HALF, (i + 1) * HALF, LANE):
            part = screen[:, c - i * HALF : c - i * HALF + LANE]
            for half in halves:
                rows = slice(half * SUB, (half + 1) * SUB)
                mask = mask_ref[rows, c : c + LANE].astype(F32)
                residual_ref[:, rows, c : c + LANE] = mask[None] * (
                    x_ref[half * tiles + c // LANE][:OWN_DATES] - part[:, None, :]
                )


def call(kernel, out_shape, in_specs, out_specs, scratch=(), flops=0, nbytes=0, vmem=VMEM_LIMIT):
    return pl.pallas_call(
        kernel,
        out_shape=out_shape,
        in_specs=in_specs,
        out_specs=out_specs,
        scratch_shapes=scratch,
        compiler_params=pltpu.CompilerParams(vmem_limit_bytes=vmem),
        cost_estimate=pl.CostEstimate(flops=flops, bytes_accessed=nbytes, transcendentals=0),
    )


def struct(*shape, dtype=F32):
    return jax.ShapeDtypeStruct(shape, dtype)


def body(phases, pairs, ref_pixel, coherent):
    send, cand = call(
        pack_kernel,
        (struct(STACK, OWN_IFGS, SUB, LANE), struct(1, LANE)),
        [full(pltpu.SMEM), full(pltpu.SMEM), full(pltpu.HBM)],
        (full(pltpu.HBM), full()),
        [
            pltpu.VMEM((STACK, OWN_IFGS, SUB, LANE), F32),
            pltpu.SemaphoreType.DMA((STACK,)),
            pltpu.SemaphoreType.DMA((STACK,)),
        ],
        nbytes=2 * 4 * OWN_IFGS * ROWS * COLS,
        vmem=BIG_LIMIT,
    )(ref_pixel, lax.axis_index(SPACE_AXES).reshape(1), phases)
    block = lax.all_to_all(send, STACK_AXES, split_axis=0, concat_axis=0, tiled=True)

    design_t = call(
        design_kernel,
        struct(DATES, IFGS, dtype=BF16),
        [full()],
        full(),
        flops=10**4,
        nbytes=10**4,
    )(pairs.T)

    refs = cand
    for axis in ("z_lo", "z_hi"):
        refs = jnp.sum(lax.all_gather(refs, axis, axis=0, tiled=True), axis=0, keepdims=True)
    refs = lax.all_gather(refs, "x_hi", axis=0, tiled=True)
    refs = call(rows_kernel, struct(STACK, LANE), [full()], full())(refs)
    mask_tile = call(
        mask_kernel, struct(SUB, LANE), [full(pltpu.SMEM), full()], full()
    )(lax.axis_index(STACK_AXES).reshape(1), coherent)
    refs, block, design_t, mask_tile = lax.optimization_barrier(
        (refs, block, design_t, mask_tile)
    )
    refs = lax.all_to_all(refs, STACK_AXES, split_axis=0, concat_axis=0, tiled=True)

    operator = call(
        operator_kernel,
        struct(DATES + OUT_ROWS + IFGS, 3 * DATES, dtype=BF16),
        [full()],
        full(),
        flops=10**4,
        nbytes=10**4,
    )(design_t)

    high, sums = call(
        invert_kernel,
        (struct(OUT_ROWS, PIXELS), struct(STACK * SUMS, LANE)),
        [full()] * 5,
        (full(), full()),
        flops=6 * 2 * PIXELS * DATES * 1200,
        nbytes=4 * (IFGS + OUT_ROWS) * PIXELS,
    )(
        block.reshape(IFGS * SUB, LANE),
        refs,
        design_t,
        operator,
        mask_tile,
    )

    count = SPACE
    tiles = COLS // LANE
    edge = HALF // LANE
    moves = []
    for s in range(STACK):
        step = -1 if s % tiles < edge else 1 if s % tiles >= tiles - edge else 0
        moves += [
            (s * count + i, s * count + i + step)
            for i in range(count)
            if step and 0 <= i + step < count
        ]
    beside = lax.ppermute(sums, STACK_AXES + SPACE_AXES, moves)

    pieces = call(
        pieces_kernel,
        struct(STACK * PIECE * SUB, LANE),
        [full()] * 2,
        full(),
        nbytes=4 * 2 * STACK * PIECE * PIXELS,
    )(high, beside)
    dated = lax.all_to_all(
        pieces.reshape(STACK, PIECE, SUB, LANE), STACK_AXES, split_axis=0, concat_axis=0, tiled=True
    )

    return call(
        screen_kernel,
        (struct(OWN_DATES, COLS), struct(OWN_DATES, ROWS, COLS)),
        [full()] * 2,
        (full(), full()),
        flops=2 * 64 * 768 * 256 * 3,
        nbytes=2 * 4 * PIECE * ROWS * COLS,
    )(dated, coherent)


def solution(mesh):
    fine = Mesh(mesh.devices.reshape(4, 2, 2, 2, 4, 4), STACK_AXES + SPACE_AXES)
    return jax.shard_map(
        body,
        mesh=fine,
        in_specs=(P(STACK_AXES, None, SPACE_AXES), P(), P(), P(None, SPACE_AXES)),
        out_specs=(P(STACK_AXES, SPACE_AXES), P(STACK_AXES, None, SPACE_AXES)),
        check_vma=False,
    )
```
